128 devices in a mesh: rows: 128 (over x, z, y, core).
Axes of the slice: x: 4, y: 4, z: 4, core: 2. Of those that a mesh axis runs over, the one named last changes fastest.
Arguments:
- slab: bfloat16 [1048576, 1024], P('rows'), may hold values from -36 to 36, as said below
- test_matrix: bfloat16 [1024, 256], replicated, may hold values from -0.1875 to 0.1875
Outputs:
- basis: float32 [1048576, 256], P('rows')
- coefficients: float32 [256, 1024], replicated
- gram_factor: float32 [256, 256], replicated
The draws below stay inside these ranges and needn't reach their ends.
Inputs may be any that keep to these rules, and one draw needn't show every extreme that they name: `slab`: Real-valued embeddings.
All inputs are finite; a program needn't handle non-finite values.
Results may differ from the reference program's by a relative error of at most 0.00035.
Values sent between devices are 32-bit elements; how exact they have to be, the bound alone decides.
A program may use at most 128 MiB of HBM per device.

```python
import jax
import jax.numpy as jnp
from jax import lax

D = 1024
K = 256
ROWS_DEV = 8192
TOKENS = 1048576
N_ROWS = 128


def draw_slab(key, part):
    key = jax.random.fold_in(key, 11)
    key_noise = jax.random.fold_in(key, 0)
    key_cols = jax.random.fold_in(key, 1)
    key_rank = jax.random.fold_in(key, 3)
    position = jnp.arange(TOKENS, dtype=jnp.float32) / TOKENS
    row_scale = jnp.exp(jnp.log(3.0) * position)[:, None]
    signal_count = K // 2
    log_span = 1.6 + 0.8 * min(D // (4 * K), 1)
    column_rank = jax.random.permutation(key_rank, D)
    jitter = jax.random.uniform(key_cols, (D,), dtype=jnp.float32)
    strong_exponent = log_span * (column_rank.astype(jnp.float32) + jitter) / signal_count
    weak_exponent = log_span + 0.2 * jitter
    exponent = jnp.where(column_rank < signal_count, strong_exponent, weak_exponent)
    col_scale = 3.0 * 10.0 ** (-exponent)
    noise = jax.random.truncated_normal(key_noise, -4.0, 4.0, (TOKENS, D), dtype=jnp.float32)
    values = noise * row_scale * col_scale[None, :]
    return values.astype(jnp.bfloat16)


def centred(own_key, extent, spread, most, kind=jnp.bfloat16):
    result = jax.random.normal(own_key, extent, jnp.float32) * spread
    return jnp.minimum(jnp.maximum(result, -most), most).astype(kind)


def setup_inputs(seed: int = 0) -> dict:
    key_list = jax.random.split(jax.random.key(seed), 3)
    slab = draw_slab(jax.random.fold_in(key_list[2], 71), 0)
    test_matrix = centred(key_list[1], (D, K), D ** -0.5, 0.1875)
    return dict(slab=slab, test_matrix=test_matrix)


def factor_pair(gram):
    lower = jnp.linalg.cholesky(gram)
    eye = jnp.eye(gram.shape[0], dtype=gram.dtype)
    return (lower, lax.linalg.triangular_solve(lower, eye, left_side=True, lower=True))

def reference(slab, test_matrix):
    sketch = jnp.dot(slab.astype(jnp.float32), test_matrix.astype(jnp.float32), preferred_element_type=jnp.float32)
    gram = jnp.dot(sketch.T, sketch, precision=lax.Precision.HIGHEST)
    lower, first_inverse = factor_pair(gram)
    gram_factor = lower / jnp.sqrt(jnp.float32(TOKENS))
    first_basis = jnp.dot(sketch, first_inverse.T, precision=lax.Precision.HIGHEST)
    second_gram = jnp.dot(first_basis.T, first_basis, precision=lax.Precision.HIGHEST)
    unused_lower, second_inverse = factor_pair(second_gram)
    orthonormal = jnp.dot(first_basis, second_inverse.T, precision=lax.Precision.HIGHEST)
    blocks_q = orthonormal.reshape(N_ROWS, ROWS_DEV, K)
    blocks_a = slab.reshape(N_ROWS, ROWS_DEV, D)

    def add_block(total, pair):
        block_q, block_a = pair
        term = jnp.dot(block_q.T, block_a.astype(total.dtype), precision=lax.Precision.HIGHEST)
        return (total + term, None)
    coefficients, unused = lax.scan(add_block, jnp.zeros((K, D), dtype=jnp.float32), (blocks_q, blocks_a))
    basis = orthonormal * jnp.sqrt(jnp.float32(TOKENS))
    return (basis, coefficients, gram_factor)
```

```python
import jax
import jax.numpy as jnp
from jax import lax
from jax.experimental import pallas as pl
from jax.experimental.pallas import tpu as pltpu
from jax.sharding import PartitionSpec as P

F32 = jnp.float32
HIGH = lax.Precision.HIGHEST
MESH = pl.DeviceIdType.MESH
NN = (((1,), (0,)), ((), ()))
NT = (((1,), (1,)), ((), ()))
TN = (((0,), (0,)), ((), ()))
CHIPS = 64
TILES = 32
PANEL = 64


def mul(left, right, dims=NN):
    return lax.dot_general(left, right, dims, precision=HIGH, preferred_element_type=F32)


def two_sum(a, b):
    total = a + b
    part = total - a
    return total, (a - (total - part)) + (b - part)


CHUNK = 1024


def sketch_kernel(slab_ref, test_ref, sketch_ref, gram_ref, proj_ref, low, cross):
    step = pl.program_id(0)

    @pl.when(step == 0)
    def _():
        gram_ref[...] = jnp.zeros_like(gram_ref)
        proj_ref[...] = jnp.zeros_like(proj_ref)
        low[...] = jnp.zeros_like(low)
        cross[...] = jnp.zeros_like(cross)

    block = slab_ref[...]
    sketch = jnp.dot(block, test_ref[...], preferred_element_type=F32)
    sketch_ref[...] = sketch
    turned = sketch.T

    most = jnp.max(jnp.abs(turned), axis=1, keepdims=True)
    magic = near_power(1.5 * most) * F32(1.5 * 2.0**16)
    one = (turned + magic) - magic
    rest = turned - one
    two = rest.astype(jnp.bfloat16)
    three = (rest - two.astype(F32)).astype(jnp.bfloat16)
    one = one.astype(jnp.bfloat16)

    def outer(left, right):
        return lax.dot_general(left, right, NT, preferred_element_type=F32)

    total, error = two_sum(gram_ref[...], outer(one, one))
    gram_ref[...] = total
    low[...] += error + outer(two, two)
    cross[...] += outer(one, two) + outer(one, three)

    upper = turned.astype(jnp.bfloat16)
    lower = (turned - upper.astype(F32)).astype(jnp.bfloat16)
    proj_ref[...] += jnp.dot(upper, block, preferred_element_type=F32) + jnp.dot(
        lower, block, preferred_element_type=F32)

    @pl.when(step == pl.num_programs(0) - 1)
    def _():
        mixed = cross[...]
        gram_ref[...] += (mixed + mixed.T) + low[...]


def sketch_all(slab, test_matrix):
    rows = slab.shape[0]
    return pl.pallas_call(
        sketch_kernel,
        grid=(rows // CHUNK,),
        out_shape=(
            jax.ShapeDtypeStruct((rows, 256), F32),
            jax.ShapeDtypeStruct((256, 256), F32),
            jax.ShapeDtypeStruct((256, 1024), F32),
        ),
        in_specs=[
            pl.BlockSpec((CHUNK, 1024), lambda i: (i, 0)),
            pl.BlockSpec((1024, 256), lambda i: (0, 0)),
        ],
        out_specs=(
            pl.BlockSpec((CHUNK, 256), lambda i: (i, 0)),
            pl.BlockSpec((256, 256), lambda i: (0, 0)),
            pl.BlockSpec((256, 1024), lambda i: (0, 0)),
        ),
        scratch_shapes=[pltpu.VMEM((256, 256), F32), pltpu.VMEM((256, 256), F32)],
        compiler_params=pltpu.CompilerParams(vmem_limit_bytes=40 * 2**20),
        name="sketch_all",
    )(slab, test_matrix)


def reduce_kernel(
    gram_ref, proj_ref, gram_out, proj_out,
    gram_pair, proj_pair, gram_half, proj_half, gram_slots, proj_slots,
    pair_send, pair_recv, part_send, part_recv, done_send, done_recv, last_send, last_recv,
):
    me = lax.axis_index("rows")
    chip = me // 2
    core = me % 2
    mate = chip * 2 + 1 - core
    other = 1 - core

    def peer(step):
        target = (chip + step) % CHIPS
        return target, target * 2 + core

    barrier = pltpu.get_barrier_semaphore()

    def greet(step, carry):
        _, device = peer(step)
        pl.semaphore_signal(barrier, inc=1, device_id=(device,), device_id_type=MESH)
        return carry

    lax.fori_loop(1, CHIPS, greet, 0)
    pl.semaphore_signal(barrier, inc=1, device_id=(mate,), device_id_type=MESH)
    pl.semaphore_wait(barrier, CHIPS)

    def rows_of(which, count):
        return pl.ds(pl.multiple_of(which * count, count), count)

    gram_swap = pltpu.make_async_remote_copy(
        src_ref=gram_ref.at[rows_of(other, 128)], dst_ref=gram_pair,
        send_sem=pair_send.at[0], recv_sem=pair_recv.at[0], device_id=(mate,), device_id_type=MESH)
    proj_swap = pltpu.make_async_remote_copy(
        src_ref=proj_ref.at[rows_of(other, 128)], dst_ref=proj_pair,
        send_sem=pair_send.at[1], recv_sem=pair_recv.at[1], device_id=(mate,), device_id_type=MESH)
    gram_swap.start()
    proj_swap.start()
    gram_swap.wait()
    gram_half[...] = gram_ref[rows_of(core, 128), :] + gram_pair[...]
    proj_swap.wait()
    proj_half[...] = proj_ref[rows_of(core, 128), :] + proj_pair[...]

    def tile_at(ref, index):
        return ref.at[
            pl.ds(pl.multiple_of((index // 2) * 8, 8), 8),
            pl.ds(pl.multiple_of((index % 2) * 128, 128), 128),
        ]

    def strip_of(index, base=0):
        return (
            pl.ds(pl.multiple_of(base + (index // 4) * 8, 8), 8),
            pl.ds(pl.multiple_of((index % 4) * 256, 256), 256),
        )

    def gram_part(target, device):
        return pltpu.make_async_remote_copy(
            src_ref=tile_at(gram_half, target), dst_ref=gram_slots.at[chip],
            send_sem=part_send.at[0], recv_sem=part_recv.at[0], device_id=(device,), device_id_type=MESH)

    def proj_part(target, device):
        return pltpu.make_async_remote_copy(
            src_ref=proj_half.at[strip_of(target)], dst_ref=proj_slots.at[chip],
            send_sem=part_send.at[1], recv_sem=part_recv.at[1], device_id=(device,), device_id_type=MESH)

    def scatter(step, carry):
        target, device = peer(step)

        @pl.when(target < TILES)
        def _():
            gram_part(target, device).start()

        proj_part(target, device).start()
        return carry

    lax.fori_loop(1, CHIPS, scatter, 0)
    owner = chip < TILES
    own_tile = chip % TILES

    gram_slots[chip] = tile_at(gram_half, own_tile)[...]
    proj_slots[chip] = proj_half[strip_of(chip)]

    def wait_bytes(ref, sem):
        pltpu.make_async_copy(ref, ref, sem).wait()

    gram_base = core * 128
    tile_rows = pl.ds(pl.multiple_of(gram_base + (own_tile // 2) * 8, 8), 8)
    tile_cols = pl.ds(pl.multiple_of((own_tile % 2) * 128, 128), 128)
    tile = gram_out.at[:, tile_rows, tile_cols]

    @pl.when(owner)
    def _():
        wait_bytes(gram_slots.at[pl.ds(0, CHIPS - 1)], part_recv.at[0])

        def add(index, pair):
            high, low = pair
            high, error = two_sum(high, gram_slots[index])
            return high, low + error

        high, low = lax.fori_loop(1, CHIPS, add, (gram_slots[0], jnp.zeros((8, 128), F32)))
        gram_out[0, tile_rows, tile_cols] = high
        gram_out[1, tile_rows, tile_cols] = low

        def share(step, carry):
            _, device = peer(step)
            pltpu.make_async_remote_copy(
                src_ref=tile, dst_ref=tile, send_sem=done_send.at[0], recv_sem=done_recv.at[0],
                device_id=(device,), device_id_type=MESH).start()
            return carry

        lax.fori_loop(1, CHIPS, share, 0)

    wait_bytes(proj_slots.at[pl.ds(0, CHIPS - 1)], part_recv.at[1])
    total = lax.fori_loop(
        1, CHIPS, lambda index, total: total + proj_slots[index], proj_slots[0])
    strip = strip_of(chip, core * 128)
    proj_out[strip] = total

    def share_proj(step, carry):
        _, device = peer(step)
        pltpu.make_async_remote_copy(
            src_ref=proj_out.at[strip], dst_ref=proj_out.at[strip],
            send_sem=done_send.at[1], recv_sem=done_recv.at[1],
            device_id=(device,), device_id_type=MESH).start()
        return carry

    lax.fori_loop(1, CHIPS, share_proj, 0)

    @pl.when(owner)
    def _():
        wait_bytes(gram_slots.at[pl.ds(0, 2 * (TILES - 1))], done_recv.at[0])

    @pl.when(jnp.logical_not(owner))
    def _():
        wait_bytes(gram_slots.at[pl.ds(0, 2 * TILES)], done_recv.at[0])

    gram_rows = rows_of(core, 128)
    gram_last = pltpu.make_async_remote_copy(
        src_ref=gram_out.at[:, gram_rows], dst_ref=gram_out.at[:, gram_rows],
        send_sem=last_send.at[0], recv_sem=last_recv.at[0], device_id=(mate,), device_id_type=MESH)
    gram_last.start()
    wait_bytes(proj_slots.at[pl.ds(0, CHIPS - 1)], done_recv.at[1])
    half_rows = rows_of(core, 128)
    proj_last = pltpu.make_async_remote_copy(
        src_ref=proj_out.at[half_rows], dst_ref=proj_out.at[half_rows],
        send_sem=last_send.at[1], recv_sem=last_recv.at[1], device_id=(mate,), device_id_type=MESH)
    proj_last.start()

    @pl.when(owner)
    def _():
        wait_bytes(gram_slots.at[pl.ds(0, TILES - 1)], part_send.at[0])
        wait_bytes(gram_slots.at[pl.ds(0, CHIPS - 1)], done_send.at[0])
        wait_bytes(gram_slots.at[pl.ds(0, CHIPS - 1)], done_send.at[0])

    @pl.when(jnp.logical_not(owner))
    def _():
        wait_bytes(gram_slots.at[pl.ds(0, TILES)], part_send.at[0])

    wait_bytes(proj_slots.at[pl.ds(0, CHIPS - 1)], part_send.at[1])
    wait_bytes(proj_slots.at[pl.ds(0, CHIPS - 1)], done_send.at[1])
    gram_last.wait()
    proj_last.wait()


def reduce_all(gram, proj):
    vmem = pl.BlockSpec(memory_space=pltpu.VMEM)
    pair = pltpu.SemaphoreType.DMA((2,))
    return pl.pallas_call(
        reduce_kernel,
        out_shape=(
            jax.ShapeDtypeStruct((2, 256, 256), F32),
            jax.ShapeDtypeStruct((256, 1024), F32),
        ),
        in_specs=[vmem, vmem],
        out_specs=(vmem, vmem),
        scratch_shapes=[
            pltpu.VMEM((128, 256), F32),
            pltpu.VMEM((128, 1024), F32),
            pltpu.VMEM((128, 256), F32),
            pltpu.VMEM((128, 1024), F32),
            pltpu.VMEM((CHIPS, 8, 128), F32),
            pltpu.VMEM((CHIPS, 8, 256), F32),
        ] + [pair] * 8,
        compiler_params=pltpu.CompilerParams(
            collective_id=0, has_side_effects=True, vmem_limit_bytes=32 * 2**20),
        name="reduce_all",
    )(gram, proj)


def near_power(value):
    big = value * F32(2.0**23)
    return (big + value) - big


def grid_slice(value, grid):
    magic = F32(1.5 * 2.0**23 * grid)
    return (value + magic) - magic


def eliminate(block, lane0):
    tiles = [block[8 * t : 8 * t + 8, :] for t in range(PANEL // 8)]
    sub = lax.broadcasted_iota(jnp.int32, (8, 128), 0)
    for k in range(PANEL):
        own, line = divmod(k, 8)
        lane = lane0 + k
        pivot = jnp.broadcast_to(tiles[own][line : line + 1, :], (8, 128))
        inverse = 1.0 / jnp.broadcast_to(pivot[:, lane : lane + 1], (8, 128))
        scaled = pivot * inverse
        for t in range(own, PANEL // 8):
            column = jnp.broadcast_to(tiles[t][:, lane : lane + 1], (8, 128))
            update = column * scaled
            if t == own:
                if line == 7:
                    continue
                update = jnp.where(sub > line, update, 0.0)
            tiles[t] = tiles[t] - update
    return jnp.concatenate(tiles, axis=0)


def factor_kernel(gram_ref, lower_ref, inverse_ref, work, upper):
    n = 256
    high = gram_ref[0]
    row = lax.broadcasted_iota(jnp.int32, (n, n), 0)
    col = lax.broadcasted_iota(jnp.int32, (n, n), 1)
    diagonal = jnp.where(row == col, high, 0.0)
    scale_col = near_power(lax.rsqrt(jnp.sum(diagonal, axis=1, keepdims=True)))
    scale_row = near_power(lax.rsqrt(jnp.sum(diagonal, axis=0, keepdims=True)))
    high = high * scale_col * scale_row
    low = gram_ref[1] * scale_col * scale_row
    eye = jnp.where(row == col, 1.0, 0.0).astype(F32)
    work[:, :n] = high
    work[:, n:] = eye

    lane = lax.broadcasted_iota(jnp.int32, (PANEL, 128), 1)
    line = lax.broadcasted_iota(jnp.int32, (PANEL, 128), 0)
    wide = lax.broadcasted_iota(jnp.int32, (PANEL, n), 1)
    for p in range(n // PANEL):
        first = PANEL * p
        lane0 = first % 128
        tile0 = first - lane0
        here = (lane >= lane0) & (lane < lane0 + PANEL)
        unit = jnp.where(lane == line + (PANEL - lane0), 1.0, 0.0).astype(F32)
        block = jnp.where(here, work[first : first + PANEL, tile0 : tile0 + 128], unit)
        block = eliminate(block, lane0)
        pivots = jnp.sum(jnp.where(lane == line + lane0, block, 0.0), axis=1, keepdims=True)
        block = block * (1.0 / jnp.sqrt(pivots))
        weights = jnp.where(here, 0.0, block)
        rows = work[first : first + PANEL, :]
        zeros = jnp.zeros((PANEL, 2 * n), F32)
        stacked = jnp.concatenate([rows, zeros] if lane0 else [zeros, rows], axis=0)
        solved = mul(weights, stacked)
        left = solved[:, :n]
        left = jnp.where(wide < first + PANEL, 0.0, left)
        right = solved[:, n:]
        if p < n // PANEL - 1:
            step = mul(left, jnp.concatenate([left, right], axis=1), TN)
            work[first + PANEL :, :] = work[first + PANEL :, :] - step[first + PANEL :, :]
        upper[first : first + PANEL, :] = left
        corner = jnp.where(here & (lane >= line + lane0), block, 0.0)
        upper[first : first + PANEL, tile0 : tile0 + 128] = (
            upper[first : first + PANEL, tile0 : tile0 + 128] + corner)
        inverse_ref[first : first + PANEL, :] = right

    lower = upper[...].T
    one = grid_slice(lower, 2.0**-7)
    rest = lower - one
    two = grid_slice(rest, 2.0**-15)
    rest = rest - two
    three = grid_slice(rest, 2.0**-23)
    lower = one + (two + three)
    one, two, three = (s.astype(jnp.bfloat16) for s in (one, two, three))

    def exact(left, right):
        return lax.dot_general(
            jnp.concatenate(left, axis=1), jnp.concatenate(right, axis=1), NT,
            preferred_element_type=F32)

    residual = high - exact([one], [one])
    residual = residual - exact([one, two], [two, one])
    residual = residual - exact([one, two, three], [three, two, one])
    residual = residual - exact([two, three], [three, two])
    residual = residual + low

    first_inverse = inverse_ref[...]
    delta = mul(mul(first_inverse, residual), first_inverse, NT)

    def half(value):
        return jnp.where(row > col, value, jnp.where(row == col, 0.5 * value, 0.0))

    x = half(delta)
    for _ in range(4):
        x = half(delta - mul(x, x, NT))
    square = mul(x, x)
    fourth = mul(square, square)
    total = first_inverse + mul(fourth, first_inverse)
    total = total + mul(square, total)
    total = total - mul(x, total)
    inverse_ref[...] = total * scale_row
    lower_ref[...] = lower * (1.0 / scale_col)


def factor(gram):
    vmem = pl.BlockSpec(memory_space=pltpu.VMEM)
    square = jax.ShapeDtypeStruct((256, 256), F32)
    return pl.pallas_call(
        factor_kernel,
        out_shape=(square, square),
        in_specs=[vmem],
        out_specs=(vmem, vmem),
        scratch_shapes=[pltpu.VMEM((256, 512), F32), pltpu.VMEM((256, 256), F32)],
        compiler_params=pltpu.CompilerParams(vmem_limit_bytes=32 * 2**20),
        name="factor",
    )(gram)


def local(slab, test_matrix):
    total_rows = lax.axis_size("rows") * slab.shape[0]
    root = jnp.sqrt(F32(total_rows))
    sketch, gram, projected = sketch_all(slab, test_matrix)
    gram, projected = reduce_all(gram, projected)
    lower, inverse = factor(gram)
    basis = lax.dot_general(sketch, inverse * root, NT, precision=HIGH)
    coefficients = lax.dot_general(inverse, projected, NN, precision=HIGH)
    return (basis, coefficients, lower / root)


def solution(mesh):
    placed = (P("rows", None), P())
    return jax.shard_map(
        local, mesh=mesh, in_specs=placed, out_specs=(P("rows", None), P(), P()), check_vma=False
    )
```

```python
import functools

import jax
import jax.numpy as jnp
from jax import lax
from jax.experimental import pallas as pl
from jax.experimental.pallas import tpu as pltpu
from jax.sharding import PartitionSpec as P

F32 = jnp.float32
HIGH = lax.Precision.HIGHEST
MESH = pl.DeviceIdType.MESH
NN = (((1,), (0,)), ((), ()))
NT = (((1,), (1,)), ((), ()))
TN = (((0,), (0,)), ((), ()))
PANEL = 64


def mul(left, right, dims=NN):
    return lax.dot_general(left, right, dims, precision=HIGH, preferred_element_type=F32)


def split(value):
    upper = value.astype(jnp.bfloat16)
    return upper, (value - upper.astype(F32)).astype(jnp.bfloat16)


def mul3(left, right, dims=NN):
    a, b = split(left)
    c, d = split(right)

    def one(x, y):
        return lax.dot_general(x, y, dims, preferred_element_type=F32)

    return one(a, c) + (one(a, d) + one(b, c))


def two_sum(a, b):
    total = a + b
    part = total - a
    return total, (a - (total - part)) + (b - part)


class Place:
    def __init__(self):
        me = lax.axis_index("rows")
        self.x = me // 32
        self.member = (me // 2) % 16
        self.core = me % 2

    def mate(self):
        return self.x * 32 + self.member * 2 + 1 - self.core

    def in_plane(self, step):
        member = (self.member + step) % 16
        return member, self.x * 32 + member * 2 + self.core

    def along_x(self, step):
        x = (self.x + step) % 4
        return x * 32 + self.member * 2 + self.core

    def signal(self):
        barrier = pltpu.get_barrier_semaphore()

        def signal(device):
            pl.semaphore_signal(barrier, inc=1, device_id=(device,), device_id_type=MESH)

        def plane(step, carry):
            signal(self.in_plane(step)[1])
            return carry

        signal(self.mate())
        lax.fori_loop(1, 16, plane, 0)
        for step in range(1, 4):
            signal(self.along_x(step))

    def wait(self):
        pl.semaphore_wait(pltpu.get_barrier_semaphore(), 19)


def eight(index):
    return pl.ds(pl.multiple_of(index * 8, 8), 8)


def half_rows(core):
    return pl.ds(pl.multiple_of(core * 128, 128), 128)


def wait_bytes(ref, sem):
    pltpu.make_async_copy(ref, ref, sem).wait()


class Reduction:
    def __init__(self, place, source, out, pair, half, plane, strip, line, send, recv, exact):
        self.place, self.source, self.out, self.pair, self.half = place, source, out, pair, half
        self.plane, self.strip, self.line = plane, strip, line
        self.send, self.recv, self.exact = send, recv, exact

    def copy(self, phase, src, dst, device):
        return pltpu.make_async_remote_copy(
            src_ref=src, dst_ref=dst, send_sem=self.send.at[phase], recv_sem=self.recv.at[phase],
            device_id=(device,), device_id_type=MESH)

    def swap(self):
        place = self.place
        return self.copy(0, self.source.at[half_rows(1 - place.core)], self.pair, place.mate())

    def start_swap(self):
        self.swap().start()

    def to_plane(self):
        place = self.place
        self.swap().wait_recv()
        self.half[...] = self.source[half_rows(place.core), :] + self.pair[...]
        self.plane[place.member] = self.half[eight(place.member), :]

        def send(step, carry):
            member, device = place.in_plane(step)
            self.copy(1, self.half.at[eight(member)], self.plane.at[place.member], device).start()
            return carry

        lax.fori_loop(1, 16, send, 0)

    def add(self, terms):
        if not self.exact:
            total = terms[0][0]
            for term in terms[1:]:
                total = total + term[0]
            return (total,)
        high, low = terms[0][0], jnp.zeros_like(terms[0][0])
        for term in terms[1:]:
            high, error = two_sum(high, term[0])
            low = low + error
        for term in terms:
            if len(term) > 1:
                low = low + term[1]
        high, low = two_sum(high, low)
        return high, low

    def to_line(self):
        place = self.place
        wait_bytes(self.plane.at[pl.ds(0, 15)], self.recv.at[1])
        for index, value in enumerate(self.add([(self.plane[t],) for t in range(16)])):
            self.strip[index] = value
            self.line[place.x, index] = value
        for step in range(1, 4):
            self.copy(2, self.strip, self.line.at[place.x], place.along_x(step)).start()

    def back_to_plane(self):
        place = self.place
        wait_bytes(self.line.at[pl.ds(0, 3)], self.recv.at[2])
        planes = self.strip.shape[0]
        rows = eight(place.core * 16 + place.member)
        terms = [[self.line[x, index] for index in range(planes)] for x in range(4)]
        for index, value in enumerate(self.add(terms)):
            self.out[index, rows, :] = value

        def send(step, carry):
            self.copy(3, self.out.at[:, rows], self.out.at[:, rows], place.in_plane(step)[1]).start()
            return carry

        lax.fori_loop(1, 16, send, 0)

    def last(self):
        place = self.place
        rows = half_rows(place.core)
        return self.copy(4, self.out.at[:, rows], self.out.at[:, rows], place.mate())

    def back_to_mate(self):
        wait_bytes(self.out.at[:, pl.ds(0, 120)], self.recv.at[3])
        self.last().start()

    def finish(self):
        self.last().wait_recv()

    def drain(self):
        self.swap().wait_send()
        wait_bytes(self.plane.at[pl.ds(0, 15)], self.send.at[1])
        wait_bytes(self.line.at[pl.ds(0, 3)], self.send.at[2])
        wait_bytes(self.out.at[:, pl.ds(0, 120)], self.send.at[3])
        self.last().wait_send()


def reduction_scratch(width, planes):
    return [
        pltpu.VMEM((128, width), F32),
        pltpu.VMEM((128, width), F32),
        pltpu.VMEM((16, 8, width), F32),
        pltpu.VMEM((planes, 8, width), F32),
        pltpu.VMEM((4, planes, 8, width), F32),
        pltpu.SemaphoreType.DMA((5,)),
        pltpu.SemaphoreType.DMA((5,)),
    ]


def near_power(value):
    big = value * F32(2.0**23)
    return (big + value) - big


def grid_slice(value, grid):
    magic = F32(1.5 * 2.0**23 * grid)
    return (value + magic) - magic


def reciprocal(value):
    guess = pl.reciprocal(value, approx=True)
    guess = guess * (2.0 - value * guess)
    return guess * (2.0 - value * guess)


def eliminate(block, lane0):
    count = PANEL // 8
    tiles = [block[8 * t : 8 * t + 8, :] for t in range(count)]
    sub = lax.broadcasted_iota(jnp.int32, (8, 128), 0)

    def spread(value, lane):
        return jnp.broadcast_to(value[:, lane : lane + 1], (8, 128))

    for own in range(count):
        lane = lane0 + 8 * own
        pivots = [jnp.broadcast_to(tiles[own][j : j + 1, :], (8, 128)) for j in range(8)]
        columns = {
            t: [spread(tiles[t], lane + j) for j in range(8)] for t in range(own + 1, count)}
        head = [[spread(pivots[i], lane + j) if j >= i else None for j in range(8)] for i in range(8)]
        scaled = []
        ratio = [[None] * 8 for _ in range(8)]
        for i in range(8):
            inverse = reciprocal(head[i][i])
            for j in range(i + 1, 8):
                ratio[i][j] = head[i][j] * inverse
                for q in range(j, 8):
                    head[j][q] = head[j][q] - ratio[i][j] * head[i][q]
                pivots[j] = pivots[j] - ratio[i][j] * pivots[i]
            scaled.append(pivots[i] * inverse)
        for t in range(own + 1, count):
            done = []
            for j in range(8):
                column = columns[t][j]
                for i in range(j):
                    column = column - done[i] * ratio[i][j]
                done.append(column)
                tiles[t] = tiles[t] - column * scaled[j]
        result = pivots[0]
        for j in range(1, 8):
            result = jnp.where(sub == j, pivots[j], result)
        tiles[own] = result
    return jnp.concatenate(tiles, axis=0)


def factor_gram(gram_ref, lower_ref, inverse_ref, work, upper, between):
    n = 256
    high = gram_ref[0]
    row = lax.broadcasted_iota(jnp.int32, (n, n), 0)
    col = lax.broadcasted_iota(jnp.int32, (n, n), 1)
    diagonal = jnp.where(row == col, high, 0.0)
    scale_col = near_power(lax.rsqrt(jnp.sum(diagonal, axis=1, keepdims=True)))
    scale_row = near_power(lax.rsqrt(jnp.sum(diagonal, axis=0, keepdims=True)))
    high = high * scale_col * scale_row
    low = gram_ref[1] * scale_col * scale_row
    eye = jnp.where(row == col, 1.0, 0.0).astype(F32)
    work[:, :n] = high
    work[:, n:] = eye

    lane = lax.broadcasted_iota(jnp.int32, (PANEL, 128), 1)
    line = lax.broadcasted_iota(jnp.int32, (PANEL, 128), 0)
    wide = lax.broadcasted_iota(jnp.int32, (PANEL, n), 1)
    for p in range(n // PANEL):
        first = PANEL * p
        lane0 = first % 128
        tile0 = first - lane0
        here = (lane >= lane0) & (lane < lane0 + PANEL)
        unit = jnp.where(lane == line + (PANEL - lane0), 1.0, 0.0).astype(F32)
        block = jnp.where(here, work[first : first + PANEL, tile0 : tile0 + 128], unit)
        block = eliminate(block, lane0)
        pivots = jnp.sum(jnp.where(lane == line + lane0, block, 0.0), axis=1, keepdims=True)
        block = block * (1.0 / jnp.sqrt(pivots))
        weights = jnp.where(here, 0.0, block)
        rows = work[first : first + PANEL, :]
        zeros = jnp.zeros((PANEL, 2 * n), F32)
        stacked = jnp.concatenate([rows, zeros] if lane0 else [zeros, rows], axis=0)
        solved = mul(weights, stacked)
        left = solved[:, :n]
        left = jnp.where(wide < first + PANEL, 0.0, left)
        right = solved[:, n:]
        if p < n // PANEL - 1:
            step = mul(left, jnp.concatenate([left, right], axis=1), TN)
            work[first + PANEL :, :] = work[first + PANEL :, :] - step[first + PANEL :, :]
        upper[first : first + PANEL, :] = left
        corner = jnp.where(here & (lane >= line + lane0), block, 0.0)
        upper[first : first + PANEL, tile0 : tile0 + 128] = (
            upper[first : first + PANEL, tile0 : tile0 + 128] + corner)
        inverse_ref[first : first + PANEL, :] = right
        between(p)

    lower = upper[...].T
    one = grid_slice(lower, 2.0**-7)
    rest = lower - one
    two = grid_slice(rest, 2.0**-15)
    rest = rest - two
    three = grid_slice(rest, 2.0**-23)
    lower = one + (two + three)
    one, two, three = (s.astype(jnp.bfloat16) for s in (one, two, three))

    def exact(left, right):
        return lax.dot_general(
            jnp.concatenate(left, axis=1), jnp.concatenate(right, axis=1), NT,
            preferred_element_type=F32)

    residual = high - exact([one], [one])
    residual = residual - exact([one, two], [two, one])
    residual = residual - exact([one, two, three], [three, two, one])
    residual = residual - exact([two, three], [three, two])
    residual = residual + low

    first_inverse = inverse_ref[...]
    delta = mul3(mul3(first_inverse, residual), first_inverse, NT)

    def half(value):
        return jnp.where(row > col, value, jnp.where(row == col, 0.5 * value, 0.0))

    x = half(delta)
    for _ in range(3):
        x = half(delta - mul3(x, x, NT))
    square = mul3(x, x)
    fourth = mul3(square, square)
    total = first_inverse + mul3(fourth, first_inverse)
    total = total + mul3(square, total)
    total = total - mul3(x, total)
    inverse_ref[...] = total * scale_row
    lower_ref[...] = lower * (1.0 / scale_col)


CHUNK = 1024
CHUNKS = 8
GROUPS = (1, 2, 2, 3)


def main_kernel(
    slab_hbm, test_ref, sketch_hbm, lower_ref, inverse_ref, proj_out,
    slab, sketch, turned, gram, low, cross, proj, gram_out, work, upper, load_sem, store_sem,
    *scratch,
):
    place = Place()
    gram_sum = Reduction(place, gram, gram_out, *scratch[:7], exact=True)
    proj_sum = Reduction(place, proj, proj_out, *scratch[7:], exact=False)

    def rows_of(index):
        return pl.ds(index * CHUNK, CHUNK)

    def load(index):
        rows = rows_of(index)
        return pltpu.make_async_copy(slab_hbm.at[rows], slab.at[rows], load_sem.at[index])

    def store(index):
        rows = rows_of(index)
        return pltpu.make_async_copy(sketch.at[rows], sketch_hbm.at[rows], store_sem.at[index])

    for index in range(CHUNKS):
        load(index).start()
    place.signal()
    gram[...] = jnp.zeros_like(gram)
    low[...] = jnp.zeros_like(low)
    cross[...] = jnp.zeros_like(cross)
    proj[...] = jnp.zeros_like(proj)

    def make_sketch(index):
        rows = rows_of(index)
        value = jnp.dot(slab[rows, :], test_ref[...], preferred_element_type=F32)
        sketch[rows, :] = value
        turned[:, rows] = value.T

    def outer(left, right):
        return lax.dot_general(left, right, NT, preferred_element_type=F32)

    def add_gram(index):
        value = turned[:, rows_of(index)]
        most = jnp.max(jnp.abs(value), axis=1, keepdims=True)
        magic = near_power(1.5 * most) * F32(1.5 * 2.0**16)
        one = (value + magic) - magic
        rest = value - one
        two, three = split(rest)
        one = one.astype(jnp.bfloat16)
        total, error = two_sum(gram[...], outer(one, one))
        gram[...] = total
        low[...] += error + outer(two, two)
        cross[...] += outer(one, two) + outer(one, three)

    def add_proj(index):
        rows = rows_of(index)
        block = slab[rows, :]
        one, two = split(turned[:, rows])
        proj[...] += jnp.dot(one, block, preferred_element_type=F32) + jnp.dot(
            two, block, preferred_element_type=F32)

    done = 0
    for count in GROUPS:
        for index in range(done, done + count):
            load(index).wait()
        for index in range(done, done + count):
            make_sketch(index)
            if index:
                add_gram(index - 1)
        done += count
    add_gram(CHUNKS - 1)
    mixed = cross[...]
    gram[...] += (mixed + mixed.T) + low[...]

    place.wait()
    gram_sum.start_swap()
    for index in range(CHUNKS):
        store(index).start()
    add_proj(0)
    add_proj(1)
    gram_sum.to_plane()
    add_proj(2)
    add_proj(3)
    gram_sum.to_line()
    add_proj(4)
    add_proj(5)
    gram_sum.back_to_plane()
    add_proj(6)
    add_proj(7)
    gram_sum.back_to_mate()
    proj_sum.start_swap()
    gram_sum.finish()

    steps = (proj_sum.to_plane, proj_sum.to_line, proj_sum.back_to_plane, proj_sum.back_to_mate)
    factor_gram(gram_out, lower_ref, inverse_ref, work, upper, lambda panel: steps[panel]())
    proj_sum.finish()
    gram_sum.drain()
    proj_sum.drain()
    for index in range(CHUNKS):
        store(index).wait()


def reduced_factors(slab, test_matrix):
    rows = slab.shape[0]
    vmem = pl.BlockSpec(memory_space=pltpu.VMEM)
    anywhere = pl.BlockSpec(memory_space=pl.ANY)
    square = jax.ShapeDtypeStruct((256, 256), F32)
    return pl.pallas_call(
        main_kernel,
        out_shape=(
            jax.ShapeDtypeStruct((rows, 256), F32),
            square,
            square,
            jax.ShapeDtypeStruct((1, 256, 1024), F32),
        ),
        in_specs=[anywhere, vmem],
        out_specs=(anywhere, vmem, vmem, vmem),
        scratch_shapes=[
            pltpu.VMEM((rows, 1024), jnp.bfloat16),
            pltpu.VMEM((rows, 256), F32),
            pltpu.VMEM((256, rows), F32),
            pltpu.VMEM((256, 256), F32),
            pltpu.VMEM((256, 256), F32),
            pltpu.VMEM((256, 256), F32),
            pltpu.VMEM((256, 1024), F32),
            pltpu.VMEM((2, 256, 256), F32),
            pltpu.VMEM((256, 512), F32),
            pltpu.VMEM((256, 256), F32),
            pltpu.SemaphoreType.DMA((CHUNKS,)),
            pltpu.SemaphoreType.DMA((CHUNKS,)),
        ] + reduction_scratch(256, 2) + reduction_scratch(1024, 1),
        compiler_params=pltpu.CompilerParams(
            collective_id=0, has_side_effects=True, vmem_limit_bytes=60 * 2**20),
        name="reduced_factors",
    )(slab, test_matrix)


def basis_kernel(root, sketch_ref, lower_ref, inverse_ref, proj_ref, basis_ref, coef_ref, factor_ref):
    @pl.when(pl.program_id(0) == 0)
    def _():
        coef_ref[...] = mul(inverse_ref[...], proj_ref[0])
        factor_ref[...] = lower_ref[...] * F32(1.0 / root)

    basis_ref[...] = mul(sketch_ref[...], inverse_ref[...] * F32(root), NT)


def outputs(sketch, lower, inverse, proj, root):
    rows = sketch.shape[0]
    square = pl.BlockSpec((256, 256), lambda i: (0, 0))
    return pl.pallas_call(
        functools.partial(basis_kernel, root),
        grid=(rows // CHUNK,),
        out_shape=(
            jax.ShapeDtypeStruct((rows, 256), F32),
            jax.ShapeDtypeStruct((256, 1024), F32),
            jax.ShapeDtypeStruct((256, 256), F32),
        ),
        in_specs=[
            pl.BlockSpec((CHUNK, 256), lambda i: (i, 0)),
            square,
            square,
            pl.BlockSpec((1, 256, 1024), lambda i: (0, 0, 0)),
        ],
        out_specs=(
            pl.BlockSpec((CHUNK, 256), lambda i: (i, 0)),
            pl.BlockSpec((256, 1024), lambda i: (0, 0)),
            square,
        ),
        compiler_params=pltpu.CompilerParams(vmem_limit_bytes=60 * 2**20),
        name="outputs",
    )(sketch, lower, inverse, proj)


def local(slab, test_matrix):
    root = float((lax.axis_size("rows") * slab.shape[0]) ** 0.5)
    sketch, lower, inverse, proj = reduced_factors(slab, test_matrix)
    return outputs(sketch, lower, inverse, proj, root)


def solution(mesh):
    placed = (P("rows", None), P())
    return jax.shard_map(
        local, mesh=mesh, in_specs=placed, out_specs=(P("rows", None), P(), P()), check_vma=False
    )
```

```python
import functools

import jax
import jax.numpy as jnp
from jax import lax
from jax.experimental import pallas as pl
from jax.experimental.pallas import tpu as pltpu
from jax.sharding import PartitionSpec as P

F32 = jnp.float32
HIGH = lax.Precision.HIGHEST
MESH = pl.DeviceIdType.MESH
NN = (((1,), (0,)), ((), ()))
NT = (((1,), (1,)), ((), ()))
TN = (((0,), (0,)), ((), ()))
PANEL = 64


def mul(left, right, dims=NN):
    return lax.dot_general(left, right, dims, precision=HIGH, preferred_element_type=F32)


def split(value):
    upper = value.astype(jnp.bfloat16)
    return upper, (value - upper.astype(F32)).astype(jnp.bfloat16)


def mul3(left, right, dims=NN):
    a, b = split(left)
    c, d = split(right)

    def one(x, y):
        return lax.dot_general(x, y, dims, preferred_element_type=F32)

    return one(a, c) + (one(a, d) + one(b, c))


def two_sum(a, b):
    total = a + b
    part = total - a
    return total, (a - (total - part)) + (b - part)


class Place:
    def __init__(self):
        me = lax.axis_index("rows")
        self.x = me // 32
        self.member = (me // 2) % 16
        self.core = me % 2

    def mate(self):
        return self.x * 32 + self.member * 2 + 1 - self.core

    def in_plane(self, step):
        member = (self.member + step) % 16
        return member, self.x * 32 + member * 2 + self.core

    def along_x(self, step):
        x = (self.x + step) % 4
        return x * 32 + self.member * 2 + self.core

    def signal(self):
        barrier = pltpu.get_barrier_semaphore()

        def signal(device):
            pl.semaphore_signal(barrier, inc=1, device_id=(device,), device_id_type=MESH)

        def plane(step, carry):
            signal(self.in_plane(step)[1])
            return carry

        signal(self.mate())
        lax.fori_loop(1, 16, plane, 0)
        for step in range(1, 4):
            signal(self.along_x(step))

    def wait(self):
        pl.semaphore_wait(pltpu.get_barrier_semaphore(), 19)


def eight(index):
    return pl.ds(pl.multiple_of(index * 8, 8), 8)


def half_rows(core):
    return pl.ds(pl.multiple_of(core * 128, 128), 128)


def wait_bytes(ref, sem):
    pltpu.make_async_copy(ref, ref, sem).wait()


class Reduction:
    def __init__(self, place, source, out, pair, half, plane, strip, line, send, recv, exact):
        self.place, self.source, self.out, self.pair, self.half = place, source, out, pair, half
        self.plane, self.strip, self.line = plane, strip, line
        self.send, self.recv, self.exact = send, recv, exact

    def copy(self, phase, src, dst, device):
        return pltpu.make_async_remote_copy(
            src_ref=src, dst_ref=dst, send_sem=self.send.at[phase], recv_sem=self.recv.at[phase],
            device_id=(device,), device_id_type=MESH)

    def swap(self):
        place = self.place
        return self.copy(0, self.source.at[half_rows(1 - place.core)], self.pair, place.mate())

    def start_swap(self):
        self.swap().start()

    def to_plane(self):
        place = self.place
        self.swap().wait_recv()
        self.half[...] = self.source[half_rows(place.core), :] + self.pair[...]
        self.plane[place.member] = self.half[eight(place.member), :]

        def send(step, carry):
            member, device = place.in_plane(step)
            self.copy(1, self.half.at[eight(member)], self.plane.at[place.member], device).start()
            return carry

        lax.fori_loop(1, 16, send, 0)

    def add(self, terms):
        if not self.exact:
            total = terms[0][0]
            for term in terms[1:]:
                total = total + term[0]
            return (total,)
        high, low = terms[0][0], jnp.zeros_like(terms[0][0])
        for term in terms[1:]:
            high, error = two_sum(high, term[0])
            low = low + error
        for term in terms:
            if len(term) > 1:
                low = low + term[1]
        high, low = two_sum(high, low)
        return high, low

    def to_line(self):
        place = self.place
        wait_bytes(self.plane.at[pl.ds(0, 15)], self.recv.at[1])
        for index, value in enumerate(self.add([(self.plane[t],) for t in range(16)])):
            self.strip[index] = value
            self.line[place.x, index] = value
        for step in range(1, 4):
            self.copy(2, self.strip, self.line.at[place.x], place.along_x(step)).start()

    def back_to_plane(self):
        place = self.place
        wait_bytes(self.line.at[pl.ds(0, 3)], self.recv.at[2])
        planes = self.strip.shape[0]
        rows = eight(place.core * 16 + place.member)
        terms = [[self.line[x, index] for index in range(planes)] for x in range(4)]
        for index, value in enumerate(self.add(terms)):
            self.out[index, rows, :] = value

        def send(step, carry):
            self.copy(3, self.out.at[:, rows], self.out.at[:, rows], place.in_plane(step)[1]).start()
            return carry

        lax.fori_loop(1, 16, send, 0)

    def last(self):
        place = self.place
        rows = half_rows(place.core)
        return self.copy(4, self.out.at[:, rows], self.out.at[:, rows], place.mate())

    def back_to_mate(self):
        wait_bytes(self.out.at[:, pl.ds(0, 120)], self.recv.at[3])
        self.last().start()

    def finish(self):
        self.last().wait_recv()

    def drain(self):
        self.swap().wait_send()
        wait_bytes(self.plane.at[pl.ds(0, 15)], self.send.at[1])
        wait_bytes(self.line.at[pl.ds(0, 3)], self.send.at[2])
        wait_bytes(self.out.at[:, pl.ds(0, 120)], self.send.at[3])
        self.last().wait_send()


def reduction_scratch(width, planes):
    return [
        pltpu.VMEM((128, width), F32),
        pltpu.VMEM((128, width), F32),
        pltpu.VMEM((16, 8, width), F32),
        pltpu.VMEM((planes, 8, width), F32),
        pltpu.VMEM((4, planes, 8, width), F32),
        pltpu.SemaphoreType.DMA((5,)),
        pltpu.SemaphoreType.DMA((5,)),
    ]


def near_power(value):
    big = value * F32(2.0**23)
    return (big + value) - big


def grid_slice(value, grid):
    magic = F32(1.5 * 2.0**23 * grid)
    return (value + magic) - magic


def reciprocal(value):
    guess = pl.reciprocal(value, approx=True)
    guess = guess * (2.0 - value * guess)
    return guess * (2.0 - value * guess)


def eliminate(block):
    count = PANEL // 8
    tiles = [block[8 * t : 8 * t + 8, :] for t in range(count)]
    sub = lax.broadcasted_iota(jnp.int32, (8, 128), 0)

    def spread(value, lane):
        return jnp.broadcast_to(value[:, lane : lane + 1], (8, 128))

    for own in range(count):
        lane = 8 * own
        pivots = [jnp.broadcast_to(tiles[own][j : j + 1, :], (8, 128)) for j in range(8)]
        columns = {
            t: [spread(tiles[t], lane + j) for j in range(8)] for t in range(own + 1, count)}
        head = [[spread(pivots[i], lane + j) if j >= i else None for j in range(8)] for i in range(8)]
        scaled = []
        ratio = [[None] * 8 for _ in range(8)]
        for i in range(8):
            inverse = reciprocal(head[i][i])
            for j in range(i + 1, 8):
                ratio[i][j] = head[i][j] * inverse
                for q in range(j, 8):
                    head[j][q] = head[j][q] - ratio[i][j] * head[i][q]
                pivots[j] = pivots[j] - ratio[i][j] * pivots[i]
            scaled.append(pivots[i] * inverse)
        for t in range(own + 1, count):
            done = []
            for j in range(8):
                column = columns[t][j]
                for i in range(j):
                    column = column - done[i] * ratio[i][j]
                done.append(column)
                tiles[t] = tiles[t] - column * scaled[j]
        result = pivots[0]
        for j in range(1, 8):
            result = jnp.where(sub == j, pivots[j], result)
        tiles[own] = result
    return jnp.concatenate(tiles, axis=0)


def factor_gram(gram_ref, lower_ref, inverse_ref, work, upper, between):
    n = 256
    high = gram_ref[0]
    row = lax.broadcasted_iota(jnp.int32, (n, n), 0)
    col = lax.broadcasted_iota(jnp.int32, (n, n), 1)
    diagonal = jnp.where(row == col, high, 0.0)
    scale_col = near_power(lax.rsqrt(jnp.sum(diagonal, axis=1, keepdims=True)))
    scale_row = near_power(lax.rsqrt(jnp.sum(diagonal, axis=0, keepdims=True)))
    high = high * scale_col * scale_row
    low = gram_ref[1] * scale_col * scale_row
    eye = jnp.where(row == col, 1.0, 0.0).astype(F32)
    work[:, :n] = high
    work[:, n:] = eye

    lane = lax.broadcasted_iota(jnp.int32, (PANEL, 128), 1)
    line = lax.broadcasted_iota(jnp.int32, (PANEL, 128), 0)
    wide = lax.broadcasted_iota(jnp.int32, (PANEL, n), 1)
    front = lane < PANEL
    unit = jnp.where(lane == line + PANEL, 1.0, 0.0).astype(F32)

    def panel_step(p, carry):
        rows = pl.ds(pl.multiple_of(PANEL * p, PANEL), PANEL)
        tile = pl.ds(pl.multiple_of((p // 2) * 128, 128), 128)
        odd = jnp.broadcast_to(p % 2, (PANEL, 128)) == 1

        def turn(value):
            return jnp.where(odd, pltpu.roll(value, PANEL, 1), value)

        block = eliminate(jnp.where(front, turn(work[rows, tile]), unit))
        pivots = jnp.sum(jnp.where(lane == line, block, 0.0), axis=1, keepdims=True)
        block = block * (1.0 / jnp.sqrt(pivots))
        weights = jnp.where(front, 0.0, block)
        stacked = jnp.concatenate([jnp.zeros((PANEL, 2 * n), F32), work[rows, :]], axis=0)
        solved = mul(weights, stacked)
        left = jnp.where(wide < PANEL * (p + 1), 0.0, solved[:, :n])
        right = solved[:, n:]
        work[...] = work[...] - mul(left, jnp.concatenate([left, right], axis=1), TN)
        upper[rows, :] = left
        upper[rows, tile] = upper[rows, tile] + turn(jnp.where(front & (lane >= line), block, 0.0))
        inverse_ref[rows, :] = right
        between(p)
        return carry

    lax.fori_loop(0, n // PANEL, panel_step, 0)

    lower = upper[...].T
    one = grid_slice(lower, 2.0**-7)
    rest = lower - one
    two = grid_slice(rest, 2.0**-15)
    rest = rest - two
    three = grid_slice(rest, 2.0**-23)
    lower = one + (two + three)
    one, two, three = (s.astype(jnp.bfloat16) for s in (one, two, three))

    def exact(left, right):
        return lax.dot_general(
            jnp.concatenate(left, axis=1), jnp.concatenate(right, axis=1), NT,
            preferred_element_type=F32)

    residual = high - exact([one], [one])
    residual = residual - exact([one, two], [two, one])
    residual = residual - exact([one, two, three], [three, two, one])
    residual = residual - exact([two, three], [three, two])
    residual = residual + low

    first_inverse = inverse_ref[...]
    delta = mul3(mul3(first_inverse, residual), first_inverse, NT)

    def half(value):
        return jnp.where(row > col, value, jnp.where(row == col, 0.5 * value, 0.0))

    x = half(delta)
    x = lax.fori_loop(0, 3, lambda _, x: half(delta - mul3(x, x, NT)), x)
    square = mul3(x, x)
    fourth = mul3(square, square)
    total = first_inverse + mul3(fourth, first_inverse)
    total = total + mul3(square, total)
    total = total - mul3(x, total)
    inverse_ref[...] = total * scale_row
    lower_ref[...] = lower * (1.0 / scale_col)


CHUNK = 1024
CHUNKS = 8
GROUPS = (1, 2, 2, 3)


def main_kernel(
    slab_hbm, test_ref, sketch, lower_ref, inverse_ref, left_out, right_out,
    slab, turned, gram, low, cross, left, right, gram_out, work, upper, load_sem,
    *scratch,
):
    place = Place()
    gram_sum = Reduction(place, gram, gram_out, *scratch[:7], exact=True)
    left_sum = Reduction(place, left, left_out, *scratch[7:14], exact=False)
    right_sum = Reduction(place, right, right_out, *scratch[14:], exact=False)

    def rows_of(index):
        return pl.ds(index * CHUNK, CHUNK)

    def load(index):
        rows = rows_of(index)
        return pltpu.make_async_copy(slab_hbm.at[rows], slab.at[rows], load_sem.at[index])

    for index in range(CHUNKS):
        load(index).start()
    place.signal()
    gram[...] = jnp.zeros_like(gram)
    low[...] = jnp.zeros_like(low)
    cross[...] = jnp.zeros_like(cross)

    def make_sketch(index):
        rows = rows_of(index)
        value = jnp.dot(slab[rows, :], test_ref[...], preferred_element_type=F32)
        sketch[rows, :] = value
        turned[:, rows] = value.T

    def outer(left, right):
        return lax.dot_general(left, right, NT, preferred_element_type=F32)

    def add_gram(index):
        value = turned[:, rows_of(index)]
        most = jnp.max(jnp.abs(value), axis=1, keepdims=True)
        magic = near_power(1.5 * most) * F32(1.5 * 2.0**16)
        one = (value + magic) - magic
        rest = value - one
        two, three = split(rest)
        one = one.astype(jnp.bfloat16)
        total, error = two_sum(gram[...], outer(one, one))
        gram[...] = total
        low[...] += error + outer(two, two)
        cross[...] += outer(one, two) + outer(one, three)

    def project(part):
        side, quarter = divmod(part, 4)
        target = (left, right)[side]
        if quarter == 0:
            target[...] = jnp.zeros_like(target)

        def add(index, carry):
            rows = pl.ds(pl.multiple_of(index * CHUNK, CHUNK), CHUNK)
            block = slab[rows, side * 512 : side * 512 + 512]
            one, two = split(turned[:, rows])
            term = jnp.dot(one, block, preferred_element_type=F32) + jnp.dot(
                two, block, preferred_element_type=F32)
            target[...] += term
            return carry

        lax.fori_loop(2 * quarter, 2 * quarter + 2, add, 0)

    done = 0
    for count in GROUPS:
        for index in range(done, done + count):
            load(index).wait()
        for index in range(done, done + count):
            make_sketch(index)
            if index:
                add_gram(index - 1)
        done += count
    add_gram(CHUNKS - 1)
    mixed = cross[...]
    gram[...] += (mixed + mixed.T) + low[...]

    place.wait()
    gram_sum.start_swap()
    project(0)
    gram_sum.to_plane()
    project(1)
    project(2)
    gram_sum.to_line()
    project(3)
    left_sum.start_swap()
    project(4)
    gram_sum.back_to_plane()
    project(5)
    left_sum.to_plane()
    project(6)
    gram_sum.back_to_mate()
    project(7)
    right_sum.start_swap()
    left_sum.to_line()
    gram_sum.finish()

    def between(panel):
        @pl.when(panel == 0)
        def _():
            right_sum.to_plane()
            left_sum.back_to_plane()

        @pl.when(panel == 1)
        def _():
            right_sum.to_line()
            left_sum.back_to_mate()

        @pl.when(panel == 2)
        def _():
            right_sum.back_to_plane()

        @pl.when(panel == 3)
        def _():
            right_sum.back_to_mate()

    factor_gram(gram_out, lower_ref, inverse_ref, work, upper, between)
    left_sum.finish()
    right_sum.finish()
    gram_sum.drain()
    left_sum.drain()
    right_sum.drain()


def reduced_factors(slab, test_matrix):
    rows = slab.shape[0]
    vmem = pl.BlockSpec(memory_space=pltpu.VMEM)
    anywhere = pl.BlockSpec(memory_space=pl.ANY)
    square = jax.ShapeDtypeStruct((256, 256), F32)
    return pl.pallas_call(
        main_kernel,
        out_shape=(
            jax.ShapeDtypeStruct((rows, 256), F32),
            square,
            square,
            jax.ShapeDtypeStruct((1, 256, 512), F32),
            jax.ShapeDtypeStruct((1, 256, 512), F32),
        ),
        in_specs=[anywhere, vmem],
        out_specs=(vmem,) * 5,
        scratch_shapes=[
            pltpu.VMEM((rows, 1024), jnp.bfloat16),
            pltpu.VMEM((256, rows), F32),
            pltpu.VMEM((256, 256), F32),
            pltpu.VMEM((256, 256), F32),
            pltpu.VMEM((256, 256), F32),
            pltpu.VMEM((256, 512), F32),
            pltpu.VMEM((256, 512), F32),
            pltpu.VMEM((2, 256, 256), F32),
            pltpu.VMEM((256, 512), F32),
            pltpu.VMEM((256, 256), F32),
            pltpu.SemaphoreType.DMA((CHUNKS,)),
        ] + reduction_scratch(256, 2) + reduction_scratch(512, 1) * 2,
        compiler_params=pltpu.CompilerParams(
            collective_id=0, has_side_effects=True, vmem_limit_bytes=36 * 2**20),
        name="reduced_factors",
    )(slab, test_matrix)


def basis_kernel(
    root, sketch_ref, lower_ref, inverse_ref, left_ref, right_ref, basis_hbm, coef_ref, factor_ref, basis, sem
):
    inverse = inverse_ref[...]
    turned = inverse.T * F32(root)
    copies = []
    for index in range(CHUNKS):
        rows = pl.ds(index * CHUNK, CHUNK)
        basis[rows, :] = mul(sketch_ref[rows, :], turned)
        copies.append(pltpu.make_async_copy(basis.at[rows], basis_hbm.at[rows], sem.at[index]))
        copies[-1].start()
    coef_ref[:, :512] = mul(inverse, left_ref[0])
    coef_ref[:, 512:] = mul(inverse, right_ref[0])
    factor_ref[...] = lower_ref[...] * F32(1.0 / root)
    for copy in copies:
        copy.wait()


def outputs(sketch, lower, inverse, left, right, root):
    rows = sketch.shape[0]
    vmem = pl.BlockSpec(memory_space=pltpu.VMEM)
    return pl.pallas_call(
        functools.partial(basis_kernel, root),
        out_shape=(
            jax.ShapeDtypeStruct((rows, 256), F32),
            jax.ShapeDtypeStruct((256, 1024), F32),
            jax.ShapeDtypeStruct((256, 256), F32),
        ),
        in_specs=[vmem] * 5,
        out_specs=(pl.BlockSpec(memory_space=pl.ANY), vmem, vmem),
        scratch_shapes=[pltpu.VMEM((rows, 256), F32), pltpu.SemaphoreType.DMA((CHUNKS,))],
        compiler_params=pltpu.CompilerParams(vmem_limit_bytes=14 * 2**20),
        name="outputs",
    )(sketch, lower, inverse, left, right)


def local(slab, test_matrix):
    root = float((lax.axis_size("rows") * slab.shape[0]) ** 0.5)
    sketch, lower, inverse, left, right = reduced_factors(slab, test_matrix)
    return outputs(sketch, lower, inverse, left, right, root)


def solution(mesh):
    placed = (P("rows", None), P())
    return jax.shard_map(
        local, mesh=mesh, in_specs=placed, out_specs=(P("rows", None), P(), P()), check_vma=False
    )
```

```python
import functools

import jax
import jax.numpy as jnp
from jax import lax
from jax.experimental import pallas as pl
from jax.experimental.pallas import tpu as pltpu
from jax.sharding import PartitionSpec as P

F32 = jnp.float32
HIGH = lax.Precision.HIGHEST
MESH = pl.DeviceIdType.MESH
NN = (((1,), (0,)), ((), ()))
NT = (((1,), (1,)), ((), ()))
TN = (((0,), (0,)), ((), ()))
PANEL = 64


def mul(left, right, dims=NN):
    return lax.dot_general(left, right, dims, precision=HIGH, preferred_element_type=F32)


def split(value):
    upper = value.astype(jnp.bfloat16)
    return upper, (value - upper.astype(F32)).astype(jnp.bfloat16)


def mul3(left, right, dims=NN):
    a, b = split(left)
    c, d = split(right)

    def one(x, y):
        return lax.dot_general(x, y, dims, preferred_element_type=F32)

    return one(a, c) + (one(a, d) + one(b, c))


def two_sum(a, b):
    total = a + b
    part = total - a
    return total, (a - (total - part)) + (b - part)


class Place:
    def __init__(self):
        me = lax.axis_index("rows")
        self.x = me // 32
        self.member = (me // 2) % 16
        self.core = me % 2

    def mate(self):
        return self.x * 32 + self.member * 2 + 1 - self.core

    def in_plane(self, step):
        member = (self.member + step) % 16
        return member, self.x * 32 + member * 2 + self.core

    def along_x(self, step):
        x = (self.x + step) % 4
        return x * 32 + self.member * 2 + self.core

    def signal(self):
        barrier = pltpu.get_barrier_semaphore()

        def signal(device):
            pl.semaphore_signal(barrier, inc=1, device_id=(device,), device_id_type=MESH)

        def plane(step, carry):
            signal(self.in_plane(step)[1])
            return carry

        signal(self.mate())
        lax.fori_loop(1, 16, plane, 0)
        for step in range(1, 4):
            signal(self.along_x(step))

    def wait(self):
        pl.semaphore_wait(pltpu.get_barrier_semaphore(), 19)


def eight(index):
    return pl.ds(pl.multiple_of(index * 8, 8), 8)


def half_rows(core):
    return pl.ds(pl.multiple_of(core * 128, 128), 128)


def wait_bytes(ref, sem):
    pltpu.make_async_copy(ref, ref, sem).wait()


class Reduction:
    def __init__(self, place, source, out, pair, half, plane, strip, line, send, recv, exact):
        self.place, self.source, self.out, self.pair, self.half = place, source, out, pair, half
        self.plane, self.strip, self.line = plane, strip, line
        self.send, self.recv, self.exact = send, recv, exact

    def copy(self, phase, src, dst, device):
        return pltpu.make_async_remote_copy(
            src_ref=src, dst_ref=dst, send_sem=self.send.at[phase], recv_sem=self.recv.at[phase],
            device_id=(device,), device_id_type=MESH)

    def swap(self):
        place = self.place
        return self.copy(0, self.source.at[half_rows(1 - place.core)], self.pair, place.mate())

    def start_swap(self):
        self.swap().start()

    def to_plane(self):
        place = self.place
        self.swap().wait_recv()
        self.half[...] = self.source[half_rows(place.core), :] + self.pair[...]
        self.plane[place.member] = self.half[eight(place.member), :]

        def send(step, carry):
            member, device = place.in_plane(step)
            self.copy(1, self.half.at[eight(member)], self.plane.at[place.member], device).start()
            return carry

        lax.fori_loop(1, 16, send, 0)

    def add(self, terms):
        if not self.exact:
            total = terms[0][0]
            for term in terms[1:]:
                total = total + term[0]
            return (total,)
        high, low = terms[0][0], jnp.zeros_like(terms[0][0])
        for term in terms[1:]:
            high, error = two_sum(high, term[0])
            low = low + error
        for term in terms:
            if len(term) > 1:
                low = low + term[1]
        high, low = two_sum(high, low)
        return high, low

    def to_line(self):
        place = self.place
        wait_bytes(self.plane.at[pl.ds(0, 15)], self.recv.at[1])
        for index, value in enumerate(self.add([(self.plane[t],) for t in range(16)])):
            self.strip[index] = value
            self.line[place.x, index] = value
        for step in range(1, 4):
            self.copy(2, self.strip, self.line.at[place.x], place.along_x(step)).start()

    def back_to_plane(self):
        place = self.place
        wait_bytes(self.line.at[pl.ds(0, 3)], self.recv.at[2])
        planes = self.strip.shape[0]
        rows = eight(place.core * 16 + place.member)
        terms = [[self.line[x, index] for index in range(planes)] for x in range(4)]
        for index, value in enumerate(self.add(terms)):
            self.out[index, rows, :] = value

        def send(step, carry):
            self.copy(3, self.out.at[:, rows], self.out.at[:, rows], place.in_plane(step)[1]).start()
            return carry

        lax.fori_loop(1, 16, send, 0)

    def last(self):
        place = self.place
        rows = half_rows(place.core)
        return self.copy(4, self.out.at[:, rows], self.out.at[:, rows], place.mate())

    def back_to_mate(self):
        wait_bytes(self.out.at[:, pl.ds(0, 120)], self.recv.at[3])
        self.last().start()

    def finish(self):
        self.last().wait_recv()

    def drain(self):
        self.swap().wait_send()
        wait_bytes(self.plane.at[pl.ds(0, 15)], self.send.at[1])
        wait_bytes(self.line.at[pl.ds(0, 3)], self.send.at[2])
        wait_bytes(self.out.at[:, pl.ds(0, 120)], self.send.at[3])
        self.last().wait_send()


def reduction_scratch(width, planes):
    return [
        pltpu.VMEM((128, width), F32),
        pltpu.VMEM((128, width), F32),
        pltpu.VMEM((16, 8, width), F32),
        pltpu.VMEM((planes, 8, width), F32),
        pltpu.VMEM((4, planes, 8, width), F32),
        pltpu.SemaphoreType.DMA((5,)),
        pltpu.SemaphoreType.DMA((5,)),
    ]


def near_power(value):
    big = value * F32(2.0**23)
    return (big + value) - big


def grid_slice(value, grid):
    magic = F32(1.5 * 2.0**23 * grid)
    return (value + magic) - magic


def reciprocal(value):
    guess = pl.reciprocal(value, approx=True)
    guess = guess * (2.0 - value * guess)
    return guess * (2.0 - value * guess)


def eliminate(block):
    count = PANEL // 8
    tiles = [block[8 * t : 8 * t + 8, :] for t in range(count)]
    sub = lax.broadcasted_iota(jnp.int32, (8, 128), 0)

    def spread(value, lane):
        return jnp.broadcast_to(value[:, lane : lane + 1], (8, 128))

    for own in range(count):
        lane = 8 * own
        pivots = [jnp.broadcast_to(tiles[own][j : j + 1, :], (8, 128)) for j in range(8)]
        columns = {
            t: [spread(tiles[t], lane + j) for j in range(8)] for t in range(own + 1, count)}
        head = [[spread(pivots[i], lane + j) if j >= i else None for j in range(8)] for i in range(8)]
        scaled = []
        ratio = [[None] * 8 for _ in range(8)]
        for i in range(8):
            inverse = reciprocal(head[i][i])
            for j in range(i + 1, 8):
                ratio[i][j] = head[i][j] * inverse
                for q in range(j, 8):
                    head[j][q] = head[j][q] - ratio[i][j] * head[i][q]
                pivots[j] = pivots[j] - ratio[i][j] * pivots[i]
            scaled.append(pivots[i] * inverse)
        for t in range(own + 1, count):
            done = []
            for j in range(8):
                column = columns[t][j]
                for i in range(j):
                    column = column - done[i] * ratio[i][j]
                done.append(column)
                tiles[t] = tiles[t] - column * scaled[j]
        result = pivots[0]
        for j in range(1, 8):
            result = jnp.where(sub == j, pivots[j], result)
        tiles[own] = result
    return jnp.concatenate(tiles, axis=0)


def factor_gram(gram_ref, lower_ref, inverse_ref, work, upper, between, late):
    n = 256
    high = gram_ref[0]
    row = lax.broadcasted_iota(jnp.int32, (n, n), 0)
    col = lax.broadcasted_iota(jnp.int32, (n, n), 1)
    diagonal = jnp.where(row == col, high, 0.0)
    scale_col = near_power(lax.rsqrt(jnp.sum(diagonal, axis=1, keepdims=True)))
    scale_row = near_power(lax.rsqrt(jnp.sum(diagonal, axis=0, keepdims=True)))
    high = high * scale_col * scale_row
    low = gram_ref[1] * scale_col * scale_row
    eye = jnp.where(row == col, 1.0, 0.0).astype(F32)
    work[:, :n] = high
    work[:, n:] = eye

    lane = lax.broadcasted_iota(jnp.int32, (PANEL, 128), 1)
    line = lax.broadcasted_iota(jnp.int32, (PANEL, 128), 0)
    wide = lax.broadcasted_iota(jnp.int32, (PANEL, n), 1)
    front = lane < PANEL
    unit = jnp.where(lane == line + PANEL, 1.0, 0.0).astype(F32)

    def panel_step(p, carry):
        rows = pl.ds(pl.multiple_of(PANEL * p, PANEL), PANEL)
        tile = pl.ds(pl.multiple_of((p // 2) * 128, 128), 128)
        odd = jnp.broadcast_to(p % 2, (PANEL, 128)) == 1

        def turn(value):
            return jnp.where(odd, pltpu.roll(value, PANEL, 1), value)

        block = eliminate(jnp.where(front, turn(work[rows, tile]), unit))
        pivots = jnp.sum(jnp.where(lane == line, block, 0.0), axis=1, keepdims=True)
        block = block * (1.0 / jnp.sqrt(pivots))
        weights = jnp.where(front, 0.0, block)
        stacked = jnp.concatenate([jnp.zeros((PANEL, 2 * n), F32), work[rows, :]], axis=0)
        solved = mul(weights, stacked)
        left = jnp.where(wide < PANEL * (p + 1), 0.0, solved[:, :n])
        right = solved[:, n:]
        work[...] = work[...] - mul(left, jnp.concatenate([left, right], axis=1), TN)
        upper[rows, :] = left
        upper[rows, tile] = upper[rows, tile] + turn(jnp.where(front & (lane >= line), block, 0.0))
        inverse_ref[rows, :] = right
        between(p)
        return carry

    lax.fori_loop(0, n // PANEL, panel_step, 0)

    lower = upper[...].T
    one = grid_slice(lower, 2.0**-7)
    rest = lower - one
    two = grid_slice(rest, 2.0**-15)
    rest = rest - two
    three = grid_slice(rest, 2.0**-23)
    lower = one + (two + three)
    one, two, three = (s.astype(jnp.bfloat16) for s in (one, two, three))

    def exact(left, right):
        return lax.dot_general(
            jnp.concatenate(left, axis=1), jnp.concatenate(right, axis=1), NT,
            preferred_element_type=F32)

    residual = high - exact([one], [one])
    residual = residual - exact([one, two], [two, one])
    residual = residual - exact([one, two, three], [three, two, one])
    residual = residual - exact([two, three], [three, two])
    residual = residual + low

    first_inverse = inverse_ref[...]
    delta = mul3(mul3(first_inverse, residual), first_inverse, NT)

    def half(value):
        return jnp.where(row > col, value, jnp.where(row == col, 0.5 * value, 0.0))

    x = half(delta)
    x = lax.fori_loop(0, 3, lambda _, x: half(delta - mul3(x, x, NT)), x)
    late()
    square = mul3(x, x)
    fourth = mul3(square, square)
    total = first_inverse + mul3(fourth, first_inverse)
    total = total + mul3(square, total)
    total = total - mul3(x, total)
    inverse_ref[...] = total * scale_row
    lower_ref[...] = lower * (1.0 / scale_col)


CHUNK = 1024
CHUNKS = 8
GROUPS = (1, 2, 2, 3)


def main_kernel(
    slab_hbm, test_hbm, sketch, lower_ref, inverse_ref, left_out, right_out,
    slab, turned, gram, low, cross, left, right, gram_out, work, upper, test_ref, load_sem, test_sem,
    *scratch,
):
    place = Place()
    gram_sum = Reduction(place, gram, gram_out, *scratch[:7], exact=True)
    left_sum = Reduction(place, left, left_out, *scratch[7:14], exact=False)
    right_sum = Reduction(place, right, right_out, *scratch[14:], exact=False)

    def rows_of(index):
        return pl.ds(index * CHUNK, CHUNK)

    def load(index):
        rows = rows_of(index)
        return pltpu.make_async_copy(slab_hbm.at[rows], slab.at[rows], load_sem.at[index])

    test_copy = pltpu.make_async_copy(test_hbm, test_ref, test_sem.at[0])
    test_copy.start()
    for index in range(CHUNKS):
        load(index).start()
    place.signal()
    gram[...] = jnp.zeros_like(gram)
    low[...] = jnp.zeros_like(low)
    cross[...] = jnp.zeros_like(cross)

    def make_sketch(index):
        rows = rows_of(index)
        value = jnp.dot(slab[rows, :], test_ref[...], preferred_element_type=F32)
        sketch[rows, :] = value
        turned[:, rows] = value.T

    def outer(left, right):
        return lax.dot_general(left, right, NT, preferred_element_type=F32)

    def add_gram(index):
        value = turned[:, rows_of(index)]
        most = jnp.max(jnp.abs(value), axis=1, keepdims=True)
        magic = near_power(1.5 * most) * F32(1.5 * 2.0**16)
        one = (value + magic) - magic
        rest = value - one
        two, three = split(rest)
        one = one.astype(jnp.bfloat16)
        total, error = two_sum(gram[...], outer(one, one))
        gram[...] = total
        low[...] += error + outer(two, two)
        cross[...] += outer(one, two) + outer(one, three)

    def project(part):
        side, quarter = divmod(part, 4)
        target = (left, right)[side]
        if quarter == 0:
            target[...] = jnp.zeros_like(target)

        def add(index, carry):
            rows = pl.ds(pl.multiple_of(index * CHUNK, CHUNK), CHUNK)
            block = slab[rows, side * 512 : side * 512 + 512]
            one, two = split(turned[:, rows])
            term = jnp.dot(one, block, preferred_element_type=F32) + jnp.dot(
                two, block, preferred_element_type=F32)
            target[...] += term
            return carry

        lax.fori_loop(2 * quarter, 2 * quarter + 2, add, 0)

    test_copy.wait()
    done = 0
    for count in GROUPS:
        for index in range(done, done + count):
            load(index).wait()
        for index in range(done, done + count):
            make_sketch(index)
            if index:
                add_gram(index - 1)
        done += count
    add_gram(CHUNKS - 1)
    mixed = cross[...]
    gram[...] += (mixed + mixed.T) + low[...]

    place.wait()
    gram_sum.start_swap()
    project(0)
    project(1)
    gram_sum.to_plane()
    project(2)
    project(3)
    left_sum.start_swap()
    gram_sum.to_line()
    project(4)
    project(5)
    gram_sum.back_to_plane()
    left_sum.to_plane()
    project(6)
    project(7)
    right_sum.start_swap()
    gram_sum.back_to_mate()
    left_sum.to_line()
    right_sum.to_plane()
    gram_sum.finish()

    def between(panel):
        @pl.when(panel == 0)
        def _():
            left_sum.back_to_plane()

        @pl.when(panel == 1)
        def _():
            right_sum.to_line()

        @pl.when(panel == 2)
        def _():
            left_sum.back_to_mate()

        @pl.when(panel == 3)
        def _():
            right_sum.back_to_plane()

    factor_gram(
        gram_out, lower_ref, inverse_ref, work, upper, between, right_sum.back_to_mate)
    left_sum.finish()
    right_sum.finish()
    gram_sum.drain()
    left_sum.drain()
    right_sum.drain()


def reduced_factors(slab, test_matrix):
    rows = slab.shape[0]
    vmem = pl.BlockSpec(memory_space=pltpu.VMEM)
    anywhere = pl.BlockSpec(memory_space=pl.ANY)
    square = jax.ShapeDtypeStruct((256, 256), F32)
    return pl.pallas_call(
        main_kernel,
        out_shape=(
            jax.ShapeDtypeStruct((rows, 256), F32),
            square,
            square,
            jax.ShapeDtypeStruct((1, 256, 512), F32),
            jax.ShapeDtypeStruct((1, 256, 512), F32),
        ),
        in_specs=[anywhere, anywhere],
        out_specs=(vmem,) * 5,
        scratch_shapes=[
            pltpu.VMEM((rows, 1024), jnp.bfloat16),
            pltpu.VMEM((256, rows), F32),
            pltpu.VMEM((256, 256), F32),
            pltpu.VMEM((256, 256), F32),
            pltpu.VMEM((256, 256), F32),
            pltpu.VMEM((256, 512), F32),
            pltpu.VMEM((256, 512), F32),
            pltpu.VMEM((2, 256, 256), F32),
            pltpu.VMEM((256, 512), F32),
            pltpu.VMEM((256, 256), F32),
            pltpu.VMEM((1024, 256), jnp.bfloat16),
            pltpu.SemaphoreType.DMA((CHUNKS,)),
            pltpu.SemaphoreType.DMA((1,)),
        ] + reduction_scratch(256, 2) + reduction_scratch(512, 1) * 2,
        compiler_params=pltpu.CompilerParams(
            collective_id=0, has_side_effects=True, vmem_limit_bytes=36 * 2**20),
        name="reduced_factors",
    )(slab, test_matrix)


def basis_kernel(
    root, sketch_ref, lower_ref, inverse_ref, left_ref, right_ref, basis_hbm, coef_ref, factor_ref, basis, sem
):
    inverse = inverse_ref[...]
    turned = inverse.T * F32(root)
    copies = []
    for index in range(CHUNKS):
        rows = pl.ds(index * CHUNK, CHUNK)
        basis[rows, :] = mul(sketch_ref[rows, :], turned)
        copies.append(pltpu.make_async_copy(basis.at[rows], basis_hbm.at[rows], sem.at[index]))
        copies[-1].start()
    coef_ref[:, :512] = mul(inverse, left_ref[0])
    coef_ref[:, 512:] = mul(inverse, right_ref[0])
    factor_ref[...] = lower_ref[...] * F32(1.0 / root)
    for copy in copies:
        copy.wait()


def outputs(sketch, lower, inverse, left, right, root):
    rows = sketch.shape[0]
    vmem = pl.BlockSpec(memory_space=pltpu.VMEM)
    return pl.pallas_call(
        functools.partial(basis_kernel, root),
        out_shape=(
            jax.ShapeDtypeStruct((rows, 256), F32),
            jax.ShapeDtypeStruct((256, 1024), F32),
            jax.ShapeDtypeStruct((256, 256), F32),
        ),
        in_specs=[vmem] * 5,
        out_specs=(pl.BlockSpec(memory_space=pl.ANY), vmem, vmem),
        scratch_shapes=[pltpu.VMEM((rows, 256), F32), pltpu.SemaphoreType.DMA((CHUNKS,))],
        compiler_params=pltpu.CompilerParams(vmem_limit_bytes=14 * 2**20),
        name="outputs",
    )(sketch, lower, inverse, left, right)


def local(slab, test_matrix):
    root = float((lax.axis_size("rows") * slab.shape[0]) ** 0.5)
    sketch, lower, inverse, left, right = reduced_factors(slab, test_matrix)
    return outputs(sketch, lower, inverse, left, right, root)


def solution(mesh):
    placed = (P("rows", None), P())
    return jax.shard_map(
        local, mesh=mesh, in_specs=placed, out_specs=(P("rows", None), P(), P()), check_vma=False
    )
```
